32 devices in a mesh: head: 4 (over z), ctx: 8 (over y, x, core).
Axes of the slice: x: 2, y: 2, z: 4, core: 2. Of those that a mesh axis runs over, the one named last changes fastest.
Arguments:
- query_input: bfloat16 [4, 16, 1536], P(None, 'ctx'), may hold values from -6 to 6
- new_latent: bfloat16 [4, 16, 512], P(None, 'ctx'), may hold values from -30 to 30
- new_rotary: bfloat16 [4, 16, 64], P(None, 'ctx'), may hold values from -6 to 6
- lengths: int32 [16], replicated, may hold values from 1 to 16384, as said below
- adapter_index: int32 [2], replicated, may hold values from 0 to 7
- query_up: bfloat16 [1536, 128, 192], P('ctx', 'head'), may hold values from -0.15625 to 0.15625
- latent_up: bfloat16 [512, 128, 256], P('ctx', 'head'), may hold values from -0.25 to 0.25
- query_adapter_down: bfloat16 [8, 1536, 64], replicated, may hold values from -0.15625 to 0.15625
- query_adapter_up: bfloat16 [8, 64, 128, 192], P(None, None, 'head'), may hold values from -0.75 to 0.75
- latent_adapter_down: bfloat16 [8, 512, 64], replicated, may hold values from -0.25 to 0.25
- latent_adapter_up: bfloat16 [8, 64, 128, 256], P(None, None, 'head'), may hold values from -0.75 to 0.75
- cache_latent: bfloat16 [16384, 512], P('ctx'), may hold values from -20 to 20
- cache_rotary: bfloat16 [64, 16384], P(None, 'ctx'), may hold values from -1200 to 1200
- output_weight: bfloat16 [16384, 7168], P('head', 'ctx'), may hold values from -0.046875 to 0.046875
Outputs:
- attention_output: bfloat16 [4, 16, 7168], P(None, 'head', 'ctx')
The draws below stay inside these ranges and needn't reach their ends.
Inputs may be any that keep to these rules, and one draw needn't show every extreme that they name: Row r attends to cached positions 0 to lengths[r] - 1; some row's length is exactly 16384.
All inputs are finite; a program needn't handle non-finite values.
Results may differ from the reference program's by a relative error of at most 0.012.
The reference program's roundings to bfloat16 on the way count: a program that leaves them out, or rounds other values in their place, can miss the bound.
Values may be sent and summed in bfloat16 or wider, within the bound.
A program may use at most 256 MiB of HBM per device.

```python
import math
import jax
import jax.numpy as jnp
from jax import lax

HEADS = 128
QUERY_RANK = 1536
LATENT = 512
NOPE_DIM = 128
ROTARY = 64
VALUE_DIM = 128
MODEL = 7168
RANK = 64
ADAPTERS = 8
STEPS = 4
ROWS = 16
CONTEXT_DEV = 2048
CONTEXT = 16384
N_CTX = 8


def draw_lengths(key, part):
    key = jax.random.fold_in(key, 23)
    first_key, second_key = jax.random.split(key, 2)
    drawn = jax.random.randint(first_key, (ROWS,), 1, CONTEXT + 1)
    longest = jax.random.randint(second_key, (), 0, ROWS)
    return jnp.where(jnp.arange(ROWS) == longest, CONTEXT, drawn).astype(jnp.int32)


def draw_cache_latent(key, part):
    key = jax.random.fold_in(key, 11)
    base_key, row_key, column_key, block_key, region_key = jax.random.split(key, 5)
    region_size = min(128, CONTEXT_DEV)
    region_count = (CONTEXT + region_size - 1) // region_size
    places = jnp.arange(CONTEXT, dtype=jnp.int32)
    owner = places // CONTEXT_DEV
    region = places // region_size
    row_scale = jnp.exp(jax.random.uniform(row_key, (CONTEXT, 1), jnp.float32, math.log(0.12), math.log(1.2)))
    column_scale = jnp.exp(jax.random.uniform(column_key, (1, LATENT), jnp.float32, math.log(0.7), math.log(1.4)))
    block_mean = jnp.clip(jax.random.normal(block_key, (N_CTX, LATENT), jnp.float32), -4.0, 4.0)
    region_mean = 0.8 * jnp.clip(jax.random.normal(region_key, (region_count, LATENT), jnp.float32), -4.0, 4.0)
    smooth = block_mean[owner] + region_mean[region]
    base = jnp.clip(jax.random.normal(base_key, (CONTEXT, LATENT), jnp.float32), -4.0, 4.0)
    return (smooth + base * row_scale * column_scale).astype(jnp.bfloat16)


def draw_cache_rotary(key, part):
    key = jax.random.fold_in(key, 31)
    base_key, scale_key, block_key, within_key, boost_key = jax.random.split(key, 5)
    places = jnp.arange(CONTEXT, dtype=jnp.int32)
    position_scale = jnp.exp(jax.random.uniform(scale_key, (CONTEXT,), jnp.float32, math.log(0.15), math.log(1.5)))
    base = jnp.clip(jax.random.normal(base_key, (ROTARY, CONTEXT), jnp.float32), -4.0, 4.0)
    spot = jax.random.randint(block_key, (), 0, N_CTX) * CONTEXT_DEV + jax.random.randint(within_key, (), 0, min(32, CONTEXT_DEV))
    boost = jnp.exp(jax.random.uniform(boost_key, (), jnp.float32, math.log(14.0), math.log(24.0)))
    factor = jnp.where(places == spot, boost, position_scale)
    result = base * factor[None, :]
    return result.astype(jnp.bfloat16)


def shard_levels(key, extent, cuts, low, largest):
    def one(position, shards_of):
        steps = jax.random.uniform(jax.random.fold_in(jax.random.fold_in(key, 6), position), (shards_of,), jnp.float32, low / len(cuts), largest / len(cuts))
        return jnp.repeat(jnp.exp(steps), extent[position] // shards_of).reshape((-1,) + (1,) * (len(extent) - position - 1))

    gain = one(*cuts[0])
    for cut in cuts[1:]:
        gain = gain * one(*cut)
    return gain


def scatter_about(stream_key, shape, spread, most, cuts=(), kind=jnp.bfloat16):
    loudness = shard_levels(stream_key, shape, cuts, -0.22, 0.18) if cuts else 1.0
    entries = jax.random.normal(stream_key, shape, jnp.float32) * spread * loudness
    return jnp.minimum(jnp.maximum(entries, -most), most).astype(kind)


def setup_inputs(seed: int = 0) -> dict:
    streams_of = jax.random.split(jax.random.key(seed), 15)
    query_input = scatter_about(streams_of[0], (STEPS, ROWS, QUERY_RANK), 1.0, 6.0, ((1, 8),))
    new_latent = scatter_about(streams_of[1], (STEPS, ROWS, LATENT), 6.0, 30.0, ((1, 8),))
    new_rotary = scatter_about(streams_of[2], (STEPS, ROWS, ROTARY), 1.0, 6.0, ((1, 8),))
    lengths = draw_lengths(jax.random.fold_in(streams_of[14], 71), 0)
    adapter_index = jax.random.randint(streams_of[4], (2,), 0, ADAPTERS).astype(jnp.int32)
    query_up = scatter_about(streams_of[5], (QUERY_RANK, HEADS, NOPE_DIM + ROTARY), QUERY_RANK ** -0.5, 0.15625, ((0, 8), (1, 4)))
    latent_up = scatter_about(streams_of[6], (LATENT, HEADS, NOPE_DIM + VALUE_DIM), LATENT ** -0.5, 0.25, ((0, 8), (1, 4)))
    query_adapter_down = scatter_about(streams_of[7], (ADAPTERS, QUERY_RANK, RANK), QUERY_RANK ** -0.5, 0.15625)
    query_adapter_up = scatter_about(streams_of[8], (ADAPTERS, RANK, HEADS, NOPE_DIM + ROTARY), RANK ** -0.5, 0.75, ((2, 4),))
    latent_adapter_down = scatter_about(streams_of[9], (ADAPTERS, LATENT, RANK), LATENT ** -0.5, 0.25)
    latent_adapter_up = scatter_about(streams_of[10], (ADAPTERS, RANK, HEADS, NOPE_DIM + VALUE_DIM), RANK ** -0.5, 0.75, ((2, 4),))
    cache_latent = draw_cache_latent(jax.random.fold_in(streams_of[14], 71), 0)
    cache_rotary = draw_cache_rotary(jax.random.fold_in(streams_of[14], 71), 0)
    output_weight = scatter_about(streams_of[13], (HEADS * VALUE_DIM, MODEL), (HEADS * VALUE_DIM) ** -0.5, 0.046875, ((0, 4), (1, 8)))
    return {"query_input": query_input, "new_latent": new_latent, "new_rotary": new_rotary, "lengths": lengths, "adapter_index": adapter_index, "query_up": query_up, "latent_up": latent_up, "query_adapter_down": query_adapter_down, "query_adapter_up": query_adapter_up, "latent_adapter_down": latent_adapter_down, "latent_adapter_up": latent_adapter_up, "cache_latent": cache_latent, "cache_rotary": cache_rotary, "output_weight": output_weight}


NEG = -1e+30

def rotate(raw, positions):
    half = raw.shape[-1] // 2
    freq = jnp.exp(jnp.arange(half, dtype=jnp.float32) * (-math.log(10000.0) / half))
    angle = positions[..., None] * freq
    cosine = jnp.cos(angle)
    sine = jnp.sin(angle)
    first = raw[..., :half]
    second = raw[..., half:]
    return jnp.concatenate([first * cosine - second * sine, second * cosine + first * sine], axis=-1)

def reference(query_input, new_latent, new_rotary, lengths, adapter_index, query_up, latent_up, query_adapter_down, query_adapter_up, latent_adapter_down, latent_adapter_up, cache_latent, cache_rotary, output_weight):
    chosen_query = adapter_index[0]
    chosen_latent = adapter_index[1]
    down_query = lax.dynamic_index_in_dim(query_adapter_down, chosen_query, 0, keepdims=False).astype(jnp.float32)
    upper_query = lax.dynamic_index_in_dim(query_adapter_up, chosen_query, 0, keepdims=False).astype(jnp.float32)
    down_latent = lax.dynamic_index_in_dim(latent_adapter_down, chosen_latent, 0, keepdims=False).astype(jnp.float32)
    upper_latent = lax.dynamic_index_in_dim(latent_adapter_up, chosen_latent, 0, keepdims=False).astype(jnp.float32)
    query_merged = (query_up.astype(jnp.float32) + jnp.einsum('qr,rhd->qhd', down_query, upper_query)).astype(jnp.bfloat16)
    latent_merged = (latent_up.astype(jnp.float32) + jnp.einsum('kr,rhd->khd', down_latent, upper_latent)).astype(jnp.bfloat16)
    positions = (lengths[None, :] + jnp.arange(STEPS, dtype=jnp.int32)[:, None]).astype(jnp.float32)
    scale = 1.0 / math.sqrt(NOPE_DIM + ROTARY)
    visible = jnp.arange(CONTEXT, dtype=jnp.int32)[None, :] < lengths[:, None]
    causal = jnp.arange(STEPS, dtype=jnp.int32)[None, :] <= jnp.arange(STEPS, dtype=jnp.int32)[:, None]
    flat_input = query_input.reshape(STEPS * ROWS, QUERY_RANK)
    new_latent_wide = new_latent.astype(jnp.float32)
    new_rotary_wide = new_rotary.astype(jnp.float32)

    def one_head(head):
        query_weight = lax.dynamic_index_in_dim(query_merged, head, 1, keepdims=False)
        latent_weight = lax.dynamic_index_in_dim(latent_merged, head, 1, keepdims=False)
        absorbed = jnp.dot(query_weight[:, :NOPE_DIM], latent_weight[:, :NOPE_DIM].T, preferred_element_type=jnp.float32).astype(jnp.bfloat16)
        query_latent = jnp.dot(flat_input, absorbed, preferred_element_type=jnp.float32).astype(jnp.bfloat16)
        raw = jnp.dot(flat_input, query_weight[:, NOPE_DIM:], preferred_element_type=jnp.float32).reshape(STEPS, ROWS, ROTARY)
        query_rotary = rotate(raw, positions).astype(jnp.bfloat16).reshape(STEPS * ROWS, ROTARY)
        cached = (jnp.dot(query_latent, cache_latent.T, preferred_element_type=jnp.float32) + jnp.dot(query_rotary, cache_rotary, preferred_element_type=jnp.float32)) * scale
        cached = jnp.where(visible[None], cached.reshape(STEPS, ROWS, CONTEXT), NEG)
        own = jnp.einsum('srk,jrk->srj', query_latent.reshape(STEPS, ROWS, LATENT).astype(jnp.float32), new_latent_wide)
        own = own + jnp.einsum('sre,jre->srj', query_rotary.reshape(STEPS, ROWS, ROTARY).astype(jnp.float32), new_rotary_wide)
        own = jnp.where(causal[:, None, :], own * scale, NEG)
        top = jnp.maximum(lax.optimization_barrier(jnp.max(cached, axis=2)), lax.optimization_barrier(jnp.max(own, axis=2)))
        cached_weight = jnp.where(visible[None], jnp.exp(cached - top[..., None]), 0.0)
        own_weight = jnp.where(causal[:, None, :], jnp.exp(own - top[..., None]), 0.0)
        total = lax.optimization_barrier(jnp.sum(cached_weight, axis=2)) + lax.optimization_barrier(jnp.sum(own_weight, axis=2))
        mixed = jnp.dot(cached_weight.astype(jnp.bfloat16).reshape(STEPS * ROWS, CONTEXT), cache_latent, preferred_element_type=jnp.float32).reshape(STEPS, ROWS, LATENT)
        own_rounded = lax.optimization_barrier(own_weight.astype(jnp.bfloat16)).astype(jnp.float32)
        mixed = mixed + jnp.einsum('srj,jrk->srk', own_rounded, new_latent_wide)
        attended = (mixed / total[..., None]).reshape(STEPS * ROWS, LATENT)
        value_wide = latent_weight[:, NOPE_DIM:].astype(jnp.float32)
        return jnp.dot(attended, value_wide, precision=lax.Precision.HIGHEST, preferred_element_type=jnp.float32).astype(jnp.bfloat16)
    per_head = lax.map(one_head, jnp.arange(HEADS, dtype=jnp.int32))
    joined = jnp.transpose(per_head, (1, 0, 2)).reshape(STEPS * ROWS, HEADS * VALUE_DIM)
    result = jnp.dot(joined, output_weight, preferred_element_type=jnp.float32).astype(jnp.bfloat16)
    return result.reshape(STEPS, ROWS, MODEL)
```

```python
import functools
import math

import jax
import jax.numpy as jnp
from jax import lax
from jax.experimental import pallas as pl
from jax.experimental.pallas import tpu as pltpu
from jax.sharding import PartitionSpec as P

LATENT = 512
NOPE_DIM = 128
ROTARY = 64


NEG = -1e30


def joined(value, axis, join):
    pieces = jax.tree.map(lambda part: lax.all_gather(part, axis), value)
    head = jax.tree.map(lambda part: part[0], pieces)
    tail = jax.tree.map(lambda part: part[1:], pieces)
    subtotal, _ = lax.scan(lambda subtotal, piece: (join(subtotal, piece), None), head, tail)
    return subtotal


def rotate(raw, positions):
    half = raw.shape[-1] // 2
    freq = jnp.exp(jnp.arange(half, dtype=jnp.float32) * (-math.log(10000.0) / half))
    angle = positions[..., None] * freq
    cosine = jnp.cos(angle)
    sine = jnp.sin(angle)
    first = raw[..., :half]
    second = raw[..., half:]
    return jnp.concatenate(
        [first * cosine - second * sine, second * cosine + first * sine], axis=-1
    )


def combine_states(first, second):
    top_first, total_first, mixed_first = first
    top_second, total_second, mixed_second = second
    top = jnp.maximum(top_first, top_second)
    factor_first = jnp.exp(top_first - top)
    factor_second = jnp.exp(top_second - top)
    total = total_first * factor_first + total_second * factor_second
    mixed = mixed_first * factor_first[..., None] + mixed_second * factor_second[..., None]
    return (top, total, mixed)


def value_project(states, value_wide):
    return jnp.einsum(
        "srhk,khv->srhv",
        states,
        value_wide,
        precision=lax.Precision.HIGHEST,
        preferred_element_type=jnp.float32,
    )


def on_device_general(
    query_input,
    new_latent,
    new_rotary,
    lengths,
    adapter_index,
    query_up,
    latent_up,
    query_adapter_down,
    query_adapter_up,
    latent_adapter_down,
    latent_adapter_up,
    cache_latent,
    cache_rotary,
    output_weight,
):
    chosen_query = adapter_index[0]
    chosen_latent = adapter_index[1]
    down_query = lax.dynamic_index_in_dim(query_adapter_down, chosen_query, 0, keepdims=False)
    upper_query = lax.dynamic_index_in_dim(query_adapter_up, chosen_query, 0, keepdims=False)
    down_latent = lax.dynamic_index_in_dim(latent_adapter_down, chosen_latent, 0, keepdims=False)
    upper_latent = lax.dynamic_index_in_dim(latent_adapter_up, chosen_latent, 0, keepdims=False)
    latent_full = lax.all_gather(latent_up, "ctx", axis=0, tiled=True)
    latent_merged = (
        latent_full.astype(jnp.float32)
        + jnp.einsum("kr,rhd->khd", down_latent, upper_latent, preferred_element_type=jnp.float32)
    ).astype(jnp.bfloat16)
    key_weight = latent_merged[:, :, :NOPE_DIM]
    value_wide = latent_merged[:, :, NOPE_DIM:].astype(jnp.float32)
    merged = (
        lax.all_gather(query_up, "ctx", axis=0, tiled=True).astype(jnp.float32)
        + jnp.einsum("nr,rhd->nhd", down_query, upper_query, preferred_element_type=jnp.float32)
    ).astype(jnp.bfloat16)
    folded = jnp.einsum(
        "nhd,khd->nhk", merged[:, :, :NOPE_DIM], key_weight, preferred_element_type=jnp.float32
    ).astype(jnp.bfloat16)
    query_map = jnp.concatenate([folded, merged[:, :, NOPE_DIM:]], axis=2)
    step_count = query_input.shape[0]
    row_count = query_input.shape[1]
    row_start = lax.axis_index("ctx") * row_count
    local_lengths = lax.dynamic_slice_in_dim(lengths, row_start, row_count, 0)
    product = jnp.einsum(
        "srq,qhe->srhe", query_input, query_map, preferred_element_type=jnp.float32
    )
    project_step_count = query_input.shape[0]
    positions = (
        local_lengths[None, :] + jnp.arange(project_step_count, dtype=jnp.int32)[:, None]
    ).astype(jnp.float32)[:, :, None]
    latent_part = product[..., :LATENT].astype(jnp.bfloat16)
    rotary_part = rotate(product[..., LATENT:], positions).astype(jnp.bfloat16)
    query_latent, query_rotary = (
        lax.all_gather(latent_part, "ctx", axis=1, tiled=True),
        lax.all_gather(rotary_part, "ctx", axis=1, tiled=True),
    )
    span = cache_latent.shape[0]
    offset = lax.axis_index("ctx") * span
    visible = (offset + jnp.arange(span, dtype=jnp.int32))[None, :] < lengths[:, None]
    scale = 1.0 / math.sqrt(NOPE_DIM + ROTARY)
    tops = []
    totals = []
    mixes = []
    for step in range(step_count):
        scores = jnp.einsum(
            "rhk,tk->rht", query_latent[step], cache_latent, preferred_element_type=jnp.float32
        )
        scores = scores + jnp.einsum(
            "rhe,et->rht", query_rotary[step], cache_rotary, preferred_element_type=jnp.float32
        )
        scores = jnp.where(visible[:, None, :], scores * scale, NEG)
        top = jnp.max(scores, axis=2)
        weight = jnp.where(visible[:, None, :], jnp.exp(scores - top[..., None]), 0.0)
        tops.append(top)
        totals.append(jnp.sum(weight, axis=2))
        mixes.append(
            jnp.einsum(
                "rht,tk->rhk",
                weight.astype(jnp.bfloat16),
                cache_latent,
                preferred_element_type=jnp.float32,
            )
        )
    top_part = jnp.stack(tops)
    total_part = jnp.stack(totals)
    mixed_part = jnp.stack(mixes)
    top_all, total_all, mixed_all = joined(
        (top_part, total_part, mixed_part), "ctx", combine_states
    )
    top_local = lax.dynamic_slice_in_dim(top_all, row_start, row_count, 1)
    total_local = lax.dynamic_slice_in_dim(total_all, row_start, row_count, 1)
    mixed_local = lax.dynamic_slice_in_dim(mixed_all, row_start, row_count, 1)
    own = jnp.einsum("srhk,jrk->srhj", latent_part, new_latent, preferred_element_type=jnp.float32)
    own = own + jnp.einsum(
        "srhe,jre->srhj", rotary_part, new_rotary, preferred_element_type=jnp.float32
    )
    causal = (
        jnp.arange(step_count, dtype=jnp.int32)[None, :]
        <= jnp.arange(step_count, dtype=jnp.int32)[:, None]
    )[:, None, None, :]
    own = jnp.where(causal, own * scale, NEG)
    top_final = jnp.maximum(top_local, jnp.max(own, axis=3))
    carried = jnp.exp(top_local - top_final)
    own_weight = jnp.where(causal, jnp.exp(own - top_final[..., None]), 0.0)
    total = total_local * carried + jnp.sum(own_weight, axis=3)
    own_mixed = jnp.einsum(
        "srhj,jrk->srhk",
        own_weight.astype(jnp.bfloat16),
        new_latent,
        preferred_element_type=jnp.float32,
    )
    attended = (mixed_local * carried[..., None] + own_mixed) / total[..., None]
    head_value = value_project(attended, value_wide)
    head_output = head_value.astype(jnp.bfloat16)
    head_flat = head_output.reshape(
        step_count, row_count, head_output.shape[2] * head_output.shape[3]
    )
    partial_out = jnp.einsum(
        "srf,fd->srd",
        lax.all_gather(head_flat, "ctx", axis=1, tiled=True),
        output_weight,
        preferred_element_type=jnp.float32,
    )
    return lax.psum_scatter(
        partial_out.astype(jnp.bfloat16), "head", scatter_dimension=1, tiled=True
    )


MESH = pl.DeviceIdType.MESH
BF16 = jnp.bfloat16
F32 = jnp.float32
VMEM_LIMIT = 56 * 2**20


def vmem():
    return pl.BlockSpec(memory_space=pltpu.VMEM)


def anywhere():
    return pl.BlockSpec(memory_space=pl.ANY)


def matmul(left, right):
    return jnp.dot(left, right, preferred_element_type=F32)


def matmul_t(left, right):
    return lax.dot_general(left, right, (((1,), (1,)), ((), ())), preferred_element_type=F32)


def remote(src, dst, send, recv, axis, peer):
    return pltpu.make_async_remote_copy(
        src_ref=src,
        dst_ref=dst,
        send_sem=send,
        recv_sem=recv,
        device_id={axis: peer},
        device_id_type=MESH,
    )


def greet(peers):
    barrier = pltpu.get_barrier_semaphore()
    for axis, peer in peers:
        pl.semaphore_signal(barrier, inc=1, device_id={axis: peer}, device_id_type=MESH)
    pl.semaphore_wait(barrier, len(peers))


def block_of(device, chips):
    return lax.rem(device, 2) * chips + device // 2


def exchange_kernel(n, chips, wl, wq, pack, cache, rotary, wl_all, wq_all, pack_all, cache_o, rotary_o, send, recv, local):
    me = lax.axis_index("ctx")
    partner = lax.bitwise_xor(me, 1)
    mine = block_of(me, chips)
    own = [
        pltpu.make_async_copy(wl.at[mine], wl_all.at[me], local.at[0]),
        pltpu.make_async_copy(wq.at[mine], wq_all.at[me], local.at[1]),
        pltpu.make_async_copy(pack, pack_all.at[me], local.at[2]),
    ]
    for copy in own:
        copy.start()
    peers = [lax.bitwise_xor(me, o) for o in range(1, n)]
    greet([("ctx", peer) for peer in peers])
    copies = []
    order = [o for o in range(n - 1, 0, -1)]
    for o in order:
        peer = peers[o - 1]
        theirs = block_of(peer, chips)
        copies.append(remote(pack, pack_all.at[me], send.at[0, o], recv.at[0, o], "ctx", peer))
        copies.append(remote(wl.at[theirs], wl_all.at[me], send.at[1, o], recv.at[1, o], "ctx", peer))
        copies.append(remote(wq.at[theirs], wq_all.at[me], send.at[2, o], recv.at[2, o], "ctx", peer))
    copies.append(remote(cache, cache_o, send.at[0, 0], recv.at[0, 0], "ctx", partner))
    copies.append(remote(rotary, rotary_o, send.at[1, 0], recv.at[1, 0], "ctx", partner))
    for copy in copies:
        copy.start()
    for copy in own:
        copy.wait()
    for copy in copies:
        copy.wait()


def query_kernel(n, half, wl, wq, qin, qin_a, qin_b, down_q, down_a, down_b, up_n, up_r, down_l, up_l, cosine, sine, q_out, v_out):
    latent = wl.shape[0] * wl.shape[2]
    weights = wl[:, 0].reshape(latent, wl.shape[3])
    weights = (weights.astype(F32) + matmul(down_l[...], up_l[0])).astype(BF16)
    nope = NOPE_DIM
    v_out[0] = weights[:, nope:]
    rank = n * 2 * half
    plain = wq[:, 0, : 2 * half].reshape(rank, nope)
    merged = (plain.astype(F32) + matmul(down_q[...], up_n[0])).astype(BF16)
    absorbed = matmul_t(merged, weights[:, :nope]).astype(BF16)
    q_out[0, :, : LATENT] = matmul(qin[...], absorbed).astype(BF16)
    turned = wq[:, 0, 2 * half :].reshape(n * half, 2 * ROTARY)
    first = (turned[:, :ROTARY].astype(F32) + matmul(down_a[...], up_r[0])).astype(BF16)
    second = (turned[:, ROTARY:].astype(F32) + matmul(down_b[...], up_r[0])).astype(BF16)
    raw = matmul(qin_a[...], first) + matmul(qin_b[...], second)
    swapped = jnp.concatenate([raw[:, ROTARY // 2 :], raw[:, : ROTARY // 2]], axis=1)
    turned_raw = raw * cosine[...] + swapped * sine[...]
    q_out[0, :, LATENT:] = jnp.concatenate(
        [turned_raw, jnp.zeros_like(turned_raw)], axis=1
    ).astype(BF16)


def attention_kernel(chips, hd, q, value, cache_a, rotary_a, cache_b, rotary_b, limit, new_key, mask, out, q_all, o_send, o_all, s_send, s_all, score_a, score_b, kept, qs, qr, os_, or_, ss, sr):
    me = lax.axis_index("ctx")
    core = lax.rem(me, 2)
    scale = 1.0 / math.sqrt(NOPE_DIM + ROTARY)
    peers = [lax.bitwise_xor(me, 2 * o) for o in range(1, chips)]
    greet([("ctx", peer) for peer in peers])
    outgoing = []
    for o in range(chips - 1, 0, -1):
        copy = remote(q, q_all.at[o - 1], qs.at[o - 1], qr.at[o - 1], "ctx", peers[o - 1])
        copy.start()
        outgoing.append(copy)
    span = cache_a.shape[0]
    rows = q.shape[0]

    def attend(query, extra):
        latent = query[:, :LATENT]
        turned = query[:, LATENT : LATENT + ROTARY]
        tops = []
        for score, cache, rotary, device in (
            (score_a, cache_a, rotary_a, me),
            (score_b, cache_b, rotary_b, lax.bitwise_xor(me, 1)),
        ):
            part = (matmul_t(latent, cache[...]) + matmul(turned, rotary[...])) * scale
            place = lax.broadcasted_iota(jnp.int32, (rows, span), 1) + device * span
            part = jnp.where(place < limit[...], part, NEG)
            score[...] = part
            tops.append(jnp.max(part, axis=1, keepdims=True))
        top = jnp.maximum(tops[0], tops[1])
        if extra:
            wide = matmul_t(query[...], new_key[...]) * scale
            wide = jnp.where(mask[...] > 0, wide, NEG)
            top = jnp.maximum(top, jnp.max(wide, axis=1, keepdims=True))
        total = jnp.zeros((rows, 1), F32)
        mixed = jnp.zeros((rows, LATENT), F32)
        seen = top > 0.5 * NEG
        for score, cache in ((score_a, cache_a), (score_b, cache_b)):
            weight = jnp.where(seen, jnp.exp(score[...] - top), 0.0)
            total = total + jnp.sum(weight, axis=1, keepdims=True)
            mixed = mixed + matmul(weight.astype(BF16), cache[...])
        if extra:
            weight = jnp.exp(wide - top)
            total = total + jnp.sum(weight, axis=1, keepdims=True)
            mixed = mixed + matmul(weight.astype(BF16), new_key[:, :LATENT])
        return top, total, mixed

    top, total, mixed = attend(q, True)
    kept[...] = mixed
    lane = lax.broadcasted_iota(jnp.int32, (rows, 128), 1)
    mine = jnp.where(lane == 0, top, total)
    s_send[chips - 1] = mine

    returns = []
    for o in range(1, chips):
        outgoing[chips - 1 - o].wait_recv()
        top_o, total_o, mixed_o = attend(q_all.at[o - 1], False)
        o_send[o - 1] = mixed_o.astype(BF16)
        s_send[o - 1] = jnp.where(lane == 0, top_o, total_o)
        for src, dst, send, recv in ((o_send, o_all, os_, or_), (s_send, s_all, ss, sr)):
            copy = remote(src.at[o - 1], dst.at[o - 1], send.at[o - 1], recv.at[o - 1], "ctx", peers[o - 1])
            copy.start()
            returns.append(copy)
    for copy in outgoing:
        copy.wait_send()
    for copy in returns:
        copy.wait()
    parts = [s_send[chips - 1]] + [s_all[o] for o in range(chips - 1)]
    best = functools.reduce(jnp.maximum, [part[:, :1] for part in parts])
    total = jnp.zeros((rows, 1), F32)
    mixed = jnp.zeros((rows, LATENT), F32)
    for index, part in enumerate(parts):
        factor = jnp.exp(part[:, :1] - best)
        total = total + part[:, 1:2] * factor
        block = kept[...] if index == 0 else o_all[index - 1].astype(F32)
        mixed = mixed + block * factor
    kept[...] = mixed / total
    each = rows // hd
    for h in range(hd):
        out[:, h * value.shape[2] : (h + 1) * value.shape[2]] = jnp.dot(
            kept[h * each : (h + 1) * each, :],
            value[h].astype(F32),
            precision=lax.Precision.HIGHEST,
            preferred_element_type=F32,
        ).astype(BF16)


def output_kernel(n, chips, nz, piece, weight, out, pieces, wide, partial, landed, ps, pr, zs, zr, ws):
    me = lax.axis_index("ctx")
    z = lax.axis_index("head")
    depth = piece.shape[1]
    loads = []
    for g in range(n):
        part = pl.ds(g * depth, depth)
        copy = pltpu.make_async_copy(weight.at[part], wide.at[part], ws.at[g])
        copy.start()
        loads.append(copy)
    peers = [lax.bitwise_xor(me, o) for o in range(1, n)]
    planes = [lax.rem(z + o, nz) for o in range(1, nz)]
    greet([("ctx", peer) for peer in peers] + [("head", plane) for plane in planes])
    mine = block_of(me, chips)
    copies = []
    for o in range(n - 1, 0, -1):
        copy = remote(piece, pieces.at[mine], ps.at[o - 1], pr.at[o - 1], "ctx", peers[o - 1])
        copy.start()
        copies.append(copy)
    pieces[mine] = piece[...]
    for copy in loads:
        copy.wait()
    for copy in copies:
        copy.wait()
    total = matmul(pieces[0], wide[:depth])
    for g in range(1, n):
        total = total + matmul(pieces[g], wide[g * depth : (g + 1) * depth])
    rows = total.shape[0] // nz
    for b in range(nz):
        partial[b] = total[b * rows : (b + 1) * rows]
    copies = []
    for o in range(1, nz):
        plane = planes[o - 1]
        copy = remote(partial.at[plane], landed.at[o - 1], zs.at[o - 1], zr.at[o - 1], "head", plane)
        copy.start()
        copies.append(copy)
    for copy in copies:
        copy.wait()
    result = partial[z]
    for o in range(nz - 1):
        result = result + landed[o]
    out[...] = result.astype(BF16)


def on_device_split(
    n,
    nz,
    query_input,
    new_latent,
    new_rotary,
    lengths,
    adapter_index,
    query_up,
    latent_up,
    query_adapter_down,
    query_adapter_up,
    latent_adapter_down,
    latent_adapter_up,
    cache_latent,
    cache_rotary,
    output_weight,
):
    chips = n // 2
    steps, local_rows, rank = query_input.shape
    rows = local_rows * n
    band = rows // nz
    heads = query_up.shape[1]
    hd = heads // n
    slab = query_up.shape[0]
    half = slab // 2
    latent_slab = latent_up.shape[0]
    value_dim = latent_up.shape[2] - NOPE_DIM
    model = output_weight.shape[1]
    count = steps * rows
    me = lax.axis_index("ctx")
    first_head = block_of(me, chips) * hd

    plain = jnp.transpose(query_up[:, :, :NOPE_DIM], (1, 0, 2))
    turned = jnp.transpose(query_up[:, :, NOPE_DIM:], (1, 0, 2))
    turned = jnp.concatenate([turned[:, :half], turned[:, half:]], axis=2)
    wq = jnp.concatenate([plain, turned], axis=1).reshape(n, hd, 3 * half, NOPE_DIM)
    wl = jnp.transpose(latent_up, (1, 0, 2)).reshape(n, hd, latent_slab, latent_up.shape[2])
    width = rank + LATENT + ROTARY
    padded = -(-width // 256) * 256
    small = jnp.concatenate([query_input, new_latent, new_rotary], axis=2)
    small = jnp.pad(small, ((0, 0), (0, 0), (0, padded - width)))
    pack = small.reshape(16, steps * local_rows * padded // 16)

    like = lambda value: jax.ShapeDtypeStruct(value.shape, value.dtype)
    wl_all, wq_all, pack_all, cache_o, rotary_o = pl.pallas_call(
        functools.partial(exchange_kernel, n, chips),
        out_shape=[
            like(wl),
            like(wq),
            jax.ShapeDtypeStruct((n,) + pack.shape, BF16),
            like(cache_latent),
            like(cache_rotary),
        ],
        in_specs=[anywhere()] * 5,
        out_specs=[anywhere()] * 5,
        scratch_shapes=[
            pltpu.SemaphoreType.DMA((3, n)),
            pltpu.SemaphoreType.DMA((3, n)),
            pltpu.SemaphoreType.DMA((3,)),
        ],
        compiler_params=pltpu.CompilerParams(collective_id=0, has_side_effects=True),
        name="exchange",
    )(wl, wq, pack, cache_latent, cache_rotary)

    def arranged(value):
        value = value.reshape((steps, nz, band) + value.shape[2:])
        value = jnp.moveaxis(value, 1, 0)
        return value.reshape((count,) + value.shape[3:])

    whole = pack_all.reshape(n, steps, local_rows, padded)
    whole = jnp.moveaxis(whole, 0, 1).reshape(steps, rows, padded)
    whole = arranged(whole)
    qin = whole[:, :rank]
    new_key = jnp.pad(whole[:, rank:width], ((0, 0), (0, ROTARY)))
    split = qin.reshape(count, n, 2, half)
    qin_a = split[:, :, 0].reshape(count, n * half)
    qin_b = split[:, :, 1].reshape(count, n * half)

    step_of = jnp.broadcast_to(jnp.arange(steps, dtype=jnp.int32)[:, None], (steps, rows))
    row_of = jnp.broadcast_to(jnp.arange(rows, dtype=jnp.int32)[None, :], (steps, rows))
    step_of = arranged(step_of)
    row_of = arranged(row_of)
    length_of = arranged(jnp.broadcast_to(lengths[None, :], (steps, rows)))
    position = (length_of + step_of).astype(F32)[:, None]
    freq = jnp.exp(
        jnp.arange(ROTARY // 2, dtype=F32) * (-math.log(10000.0) / (ROTARY // 2))
    )
    angle = position * freq
    cosine = jnp.concatenate([jnp.cos(angle)] * 2, axis=1)
    sine = jnp.concatenate([-jnp.sin(angle), jnp.sin(angle)], axis=1)
    mask = (row_of[:, None] == row_of[None, :]) & (step_of[None, :] <= step_of[:, None])
    mask = jnp.tile(mask.astype(jnp.int32), (hd, 1))
    limit = jnp.tile(length_of[:, None], (hd, 1))

    chosen_query = adapter_index[0]
    chosen_latent = adapter_index[1]
    pick = lambda value, index: lax.dynamic_index_in_dim(value, index, 0, keepdims=False)
    down_q = pick(query_adapter_down, chosen_query)
    down_l = pick(latent_adapter_down, chosen_latent)
    width_r = down_q.shape[1]

    def own_heads(value, index):
        taken = lax.dynamic_slice(
            value, (index, 0, first_head, 0), (1, width_r, hd, value.shape[3])
        )[0]
        return jnp.transpose(taken, (1, 0, 2))

    up_q = own_heads(query_adapter_up, chosen_query)
    up_l = own_heads(latent_adapter_up, chosen_latent)
    down_split = down_q.reshape(n, 2, half, width_r)
    down_a = down_split[:, 0].reshape(n * half, width_r)
    down_b = down_split[:, 1].reshape(n * half, width_r)

    per_head = lambda value: pl.BlockSpec(
        (1,) + value.shape[1:], lambda h: (h,) + (0,) * (value.ndim - 1)
    )
    same = lambda value: pl.BlockSpec(value.shape, lambda h: (0,) * value.ndim)
    up_n, up_r = up_q[:, :, :NOPE_DIM], up_q[:, :, NOPE_DIM:]
    key_width = LATENT + 2 * ROTARY
    q, value = pl.pallas_call(
        functools.partial(query_kernel, n, half),
        grid=(hd,),
        in_specs=[
            pl.BlockSpec((n, 1) + wl.shape[2:], lambda h: (0, h, 0, 0)),
            pl.BlockSpec((n, 1) + wq.shape[2:], lambda h: (0, h, 0, 0)),
            same(qin),
            same(qin_a),
            same(qin_b),
            same(down_q),
            same(down_a),
            same(down_b),
            per_head(up_n),
            per_head(up_r),
            same(down_l),
            per_head(up_l),
            same(cosine),
            same(sine),
        ],
        out_specs=[
            pl.BlockSpec((1, count, key_width), lambda h: (h, 0, 0)),
            pl.BlockSpec((1, n * latent_slab, value_dim), lambda h: (h, 0, 0)),
        ],
        out_shape=[
            jax.ShapeDtypeStruct((hd, count, key_width), BF16),
            jax.ShapeDtypeStruct((hd, n * latent_slab, value_dim), BF16),
        ],
        compiler_params=pltpu.CompilerParams(vmem_limit_bytes=VMEM_LIMIT),
        name="queries",
    )(wl_all, wq_all, qin, qin_a, qin_b, down_q, down_a, down_b, up_n, up_r, down_l, up_l, cosine, sine)
    q = q.reshape(hd * count, key_width)

    lines = hd * count
    others = chips - 1
    span = cache_latent.shape[0]
    dma = lambda number: pltpu.SemaphoreType.DMA((number,))
    piece = pl.pallas_call(
        functools.partial(attention_kernel, chips, hd),
        out_shape=jax.ShapeDtypeStruct((count, hd * value_dim), BF16),
        in_specs=[vmem()] * 9,
        out_specs=vmem(),
        scratch_shapes=[
            pltpu.VMEM((others, lines, key_width), BF16),
            pltpu.VMEM((others, lines, LATENT), BF16),
            pltpu.VMEM((others, lines, LATENT), BF16),
            pltpu.VMEM((chips, lines, 128), F32),
            pltpu.VMEM((others, lines, 128), F32),
            pltpu.VMEM((lines, span), F32),
            pltpu.VMEM((lines, span), F32),
            pltpu.VMEM((lines, LATENT), F32),
        ]
        + [dma(others)] * 6,
        compiler_params=pltpu.CompilerParams(
            collective_id=1, has_side_effects=True, vmem_limit_bytes=VMEM_LIMIT
        ),
        name="attention",
    )(q, value, cache_latent, cache_rotary, cache_o, rotary_o, limit, new_key, mask)

    result = pl.pallas_call(
        functools.partial(output_kernel, n, chips, nz),
        out_shape=jax.ShapeDtypeStruct((count // nz, model), BF16),
        in_specs=[vmem(), anywhere()],
        out_specs=vmem(),
        scratch_shapes=[
            pltpu.VMEM((n, count, hd * value_dim), BF16),
            pltpu.VMEM(output_weight.shape, BF16),
            pltpu.VMEM((nz, count // nz, model), F32),
            pltpu.VMEM((nz - 1, count // nz, model), F32),
            dma(n - 1),
            dma(n - 1),
            dma(nz - 1),
            dma(nz - 1),
            dma(n),
        ],
        compiler_params=pltpu.CompilerParams(
            collective_id=2, has_side_effects=True, vmem_limit_bytes=VMEM_LIMIT
        ),
        name="output",
    )(piece, output_weight)
    return result.reshape(steps, band, model)


def on_device(n, nz, *arrays):
    rows = arrays[0].shape[1] * n
    heads = arrays[5].shape[1]
    power = n >= 4 and n & (n - 1) == 0
    if power and nz > 1 and heads % n == 0 and rows % nz == 0 and rows * arrays[0].shape[0] // nz % 16 == 0:
        return on_device_split(n, nz, *arrays)
    return on_device_general(*arrays)


def solution(mesh):
    placed = (
        P(None, "ctx", None),
        P(None, "ctx", None),
        P(None, "ctx", None),
        P(),
        P(),
        P("ctx", "head", None),
        P("ctx", "head", None),
        P(),
        P(None, None, "head", None),
        P(),
        P(None, None, "head", None),
        P("ctx", None),
        P(None, "ctx"),
        P("head", "ctx"),
    )
    return jax.shard_map(
        functools.partial(on_device, mesh.shape["ctx"], mesh.shape["head"]),
        mesh=mesh, in_specs=placed, out_specs=P(None, "head", "ctx"), check_vma=False
    )
```

```python
import functools
import math

import jax
import jax.numpy as jnp
from jax import lax
from jax.experimental import pallas as pl
from jax.experimental.pallas import tpu as pltpu
from jax.sharding import PartitionSpec as P

LATENT = 512
NOPE_DIM = 128
ROTARY = 64


NEG = -1e30


def joined(value, axis, join):
    pieces = jax.tree.map(lambda part: lax.all_gather(part, axis), value)
    head = jax.tree.map(lambda part: part[0], pieces)
    tail = jax.tree.map(lambda part: part[1:], pieces)
    subtotal, _ = lax.scan(lambda subtotal, piece: (join(subtotal, piece), None), head, tail)
    return subtotal


def rotate(raw, positions):
    half = raw.shape[-1] // 2
    freq = jnp.exp(jnp.arange(half, dtype=jnp.float32) * (-math.log(10000.0) / half))
    angle = positions[..., None] * freq
    cosine = jnp.cos(angle)
    sine = jnp.sin(angle)
    first = raw[..., :half]
    second = raw[..., half:]
    return jnp.concatenate(
        [first * cosine - second * sine, second * cosine + first * sine], axis=-1
    )


def combine_states(first, second):
    top_first, total_first, mixed_first = first
    top_second, total_second, mixed_second = second
    top = jnp.maximum(top_first, top_second)
    factor_first = jnp.exp(top_first - top)
    factor_second = jnp.exp(top_second - top)
    total = total_first * factor_first + total_second * factor_second
    mixed = mixed_first * factor_first[..., None] + mixed_second * factor_second[..., None]
    return (top, total, mixed)


def value_project(states, value_wide):
    return jnp.einsum(
        "srhk,khv->srhv",
        states,
        value_wide,
        precision=lax.Precision.HIGHEST,
        preferred_element_type=jnp.float32,
    )


def on_device_general(
    query_input,
    new_latent,
    new_rotary,
    lengths,
    adapter_index,
    query_up,
    latent_up,
    query_adapter_down,
    query_adapter_up,
    latent_adapter_down,
    latent_adapter_up,
    cache_latent,
    cache_rotary,
    output_weight,
):
    chosen_query = adapter_index[0]
    chosen_latent = adapter_index[1]
    down_query = lax.dynamic_index_in_dim(query_adapter_down, chosen_query, 0, keepdims=False)
    upper_query = lax.dynamic_index_in_dim(query_adapter_up, chosen_query, 0, keepdims=False)
    down_latent = lax.dynamic_index_in_dim(latent_adapter_down, chosen_latent, 0, keepdims=False)
    upper_latent = lax.dynamic_index_in_dim(latent_adapter_up, chosen_latent, 0, keepdims=False)
    latent_full = lax.all_gather(latent_up, "ctx", axis=0, tiled=True)
    latent_merged = (
        latent_full.astype(jnp.float32)
        + jnp.einsum("kr,rhd->khd", down_latent, upper_latent, preferred_element_type=jnp.float32)
    ).astype(jnp.bfloat16)
    key_weight = latent_merged[:, :, :NOPE_DIM]
    value_wide = latent_merged[:, :, NOPE_DIM:].astype(jnp.float32)
    merged = (
        lax.all_gather(query_up, "ctx", axis=0, tiled=True).astype(jnp.float32)
        + jnp.einsum("nr,rhd->nhd", down_query, upper_query, preferred_element_type=jnp.float32)
    ).astype(jnp.bfloat16)
    folded = jnp.einsum(
        "nhd,khd->nhk", merged[:, :, :NOPE_DIM], key_weight, preferred_element_type=jnp.float32
    ).astype(jnp.bfloat16)
    query_map = jnp.concatenate([folded, merged[:, :, NOPE_DIM:]], axis=2)
    step_count = query_input.shape[0]
    row_count = query_input.shape[1]
    row_start = lax.axis_index("ctx") * row_count
    local_lengths = lax.dynamic_slice_in_dim(lengths, row_start, row_count, 0)
    product = jnp.einsum(
        "srq,qhe->srhe", query_input, query_map, preferred_element_type=jnp.float32
    )
    project_step_count = query_input.shape[0]
    positions = (
        local_lengths[None, :] + jnp.arange(project_step_count, dtype=jnp.int32)[:, None]
    ).astype(jnp.float32)[:, :, None]
    latent_part = product[..., :LATENT].astype(jnp.bfloat16)
    rotary_part = rotate(product[..., LATENT:], positions).astype(jnp.bfloat16)
    query_latent, query_rotary = (
        lax.all_gather(latent_part, "ctx", axis=1, tiled=True),
        lax.all_gather(rotary_part, "ctx", axis=1, tiled=True),
    )
    span = cache_latent.shape[0]
    offset = lax.axis_index("ctx") * span
    visible = (offset + jnp.arange(span, dtype=jnp.int32))[None, :] < lengths[:, None]
    scale = 1.0 / math.sqrt(NOPE_DIM + ROTARY)
    tops = []
    totals = []
    mixes = []
    for step in range(step_count):
        scores = jnp.einsum(
            "rhk,tk->rht", query_latent[step], cache_latent, preferred_element_type=jnp.float32
        )
        scores = scores + jnp.einsum(
            "rhe,et->rht", query_rotary[step], cache_rotary, preferred_element_type=jnp.float32
        )
        scores = jnp.where(visible[:, None, :], scores * scale, NEG)
        top = jnp.max(scores, axis=2)
        weight = jnp.where(visible[:, None, :], jnp.exp(scores - top[..., None]), 0.0)
        tops.append(top)
        totals.append(jnp.sum(weight, axis=2))
        mixes.append(
            jnp.einsum(
                "rht,tk->rhk",
                weight.astype(jnp.bfloat16),
                cache_latent,
                preferred_element_type=jnp.float32,
            )
        )
    top_part = jnp.stack(tops)
    total_part = jnp.stack(totals)
    mixed_part = jnp.stack(mixes)
    top_all, total_all, mixed_all = joined(
        (top_part, total_part, mixed_part), "ctx", combine_states
    )
    top_local = lax.dynamic_slice_in_dim(top_all, row_start, row_count, 1)
    total_local = lax.dynamic_slice_in_dim(total_all, row_start, row_count, 1)
    mixed_local = lax.dynamic_slice_in_dim(mixed_all, row_start, row_count, 1)
    own = jnp.einsum("srhk,jrk->srhj", latent_part, new_latent, preferred_element_type=jnp.float32)
    own = own + jnp.einsum(
        "srhe,jre->srhj", rotary_part, new_rotary, preferred_element_type=jnp.float32
    )
    causal = (
        jnp.arange(step_count, dtype=jnp.int32)[None, :]
        <= jnp.arange(step_count, dtype=jnp.int32)[:, None]
    )[:, None, None, :]
    own = jnp.where(causal, own * scale, NEG)
    top_final = jnp.maximum(top_local, jnp.max(own, axis=3))
    carried = jnp.exp(top_local - top_final)
    own_weight = jnp.where(causal, jnp.exp(own - top_final[..., None]), 0.0)
    total = total_local * carried + jnp.sum(own_weight, axis=3)
    own_mixed = jnp.einsum(
        "srhj,jrk->srhk",
        own_weight.astype(jnp.bfloat16),
        new_latent,
        preferred_element_type=jnp.float32,
    )
    attended = (mixed_local * carried[..., None] + own_mixed) / total[..., None]
    head_value = value_project(attended, value_wide)
    head_output = head_value.astype(jnp.bfloat16)
    head_flat = head_output.reshape(
        step_count, row_count, head_output.shape[2] * head_output.shape[3]
    )
    partial_out = jnp.einsum(
        "srf,fd->srd",
        lax.all_gather(head_flat, "ctx", axis=1, tiled=True),
        output_weight,
        preferred_element_type=jnp.float32,
    )
    return lax.psum_scatter(
        partial_out.astype(jnp.bfloat16), "head", scatter_dimension=1, tiled=True
    )


MESH = pl.DeviceIdType.MESH
BF16 = jnp.bfloat16
F32 = jnp.float32
VMEM_LIMIT = 56 * 2**20


def vmem():
    return pl.BlockSpec(memory_space=pltpu.VMEM)


def anywhere():
    return pl.BlockSpec(memory_space=pl.ANY)


def matmul(left, right):
    return jnp.dot(left, right, preferred_element_type=F32)


def matmul_t(left, right):
    return lax.dot_general(left, right, (((1,), (1,)), ((), ())), preferred_element_type=F32)


def remote(src, dst, send, recv, axis, peer):
    return pltpu.make_async_remote_copy(
        src_ref=src,
        dst_ref=dst,
        send_sem=send,
        recv_sem=recv,
        device_id={axis: peer},
        device_id_type=MESH,
    )


def greet(peers):
    barrier = pltpu.get_barrier_semaphore()
    for axis, peer in peers:
        pl.semaphore_signal(barrier, inc=1, device_id={axis: peer}, device_id_type=MESH)
    pl.semaphore_wait(barrier, len(peers))


def block_of(device, chips):
    return lax.rem(device, 2) * chips + device // 2


def fused_kernel(
    n, chips, nz, hd,
    key, plain, turned, pack, val, cache, rotary, weight, down_q, up_q, down_l, up_l, cosine, sine, limit, mask,
    out,
    key_all, plain_all, turned_all, pack_all, val_all, cache_o, rotary_o, wide, q, q_all, o_send, o_all, s_send, s_all,
    s_own, score_a, score_b, kept, piece, pieces, partial, landed, qin, new_key,
    ks, kr, ws, wr, ts, tr, ps, pr, vs, vr, cs, cr, qs, qr, os_, or_, ss, sr, hs, hr, zs, zr, local, loads_sem,
):
    me = lax.axis_index("ctx")
    z = lax.axis_index("head")
    partner = lax.bitwise_xor(me, 1)
    mine = block_of(me, chips)
    groups = hd // 2
    scale = 1.0 / math.sqrt(NOPE_DIM + ROTARY)
    span = cache_o.shape[0]
    count = cosine.shape[0]
    rows = 2 * count
    rank = down_q.shape[0]
    latent = down_l.shape[0]

    own = [
        pltpu.make_async_copy(key.at[mine], key_all.at[me], local.at[0]),
        pltpu.make_async_copy(plain.at[mine], plain_all.at[me], local.at[1]),
        pltpu.make_async_copy(turned.at[mine], turned_all.at[me], local.at[2]),
        pltpu.make_async_copy(pack, pack_all.at[me], local.at[3]),
        pltpu.make_async_copy(val.at[mine], val_all.at[me], local.at[4]),
    ]
    for copy in own:
        copy.start()
    peers = [lax.bitwise_xor(me, o) for o in range(1, n)]
    planes = [lax.rem(z + o, nz) for o in range(1, nz)]
    greet([("ctx", peer) for peer in peers] + [("head", plane) for plane in planes])

    order = range(n - 1, 0, -1)
    swaps = [
        remote(cache, cache_o, cs.at[0], cr.at[0], "ctx", partner),
        remote(rotary, rotary_o, cs.at[1], cr.at[1], "ctx", partner),
    ]
    firsts = []
    for o in order:
        peer = peers[o - 1]
        firsts.append(remote(pack, pack_all.at[me], ps.at[o], pr.at[o], "ctx", peer))
        firsts.append(remote(key.at[block_of(peer, chips)], key_all.at[me], ks.at[o], kr.at[o], "ctx", peer))

    def group_copies(g):
        heads = pl.ds(g * 2, 2)
        copies = []
        for o in order:
            peer = peers[o - 1]
            theirs = block_of(peer, chips)
            copies.append(
                remote(plain.at[theirs, heads], plain_all.at[me, heads], ws.at[g, o], wr.at[g, o], "ctx", peer)
            )
            copies.append(
                remote(turned.at[theirs, heads], turned_all.at[me, heads], ts.at[g, o], tr.at[g, o], "ctx", peer)
            )
        return copies

    values = [
        remote(val.at[block_of(peers[o - 1], chips)], val_all.at[me], vs.at[o], vr.at[o], "ctx", peers[o - 1])
        for o in order
    ]
    for copy in firsts:
        copy.start()
    for g in range(groups):
        for copy in group_copies(g):
            copy.start()
        if g == 0:
            for copy in swaps:
                copy.start()
    for copy in values:
        copy.start()
    loads = []
    depth = piece.shape[1]
    for g in range(n):
        part = pl.ds(g * depth, depth)
        copy = pltpu.make_async_copy(weight.at[part], wide.at[part], loads_sem.at[g])
        copy.start()
        loads.append(copy)

    for copy in own:
        copy.wait()
    for copy in firsts:
        copy.wait()
    small = pack_all[...].reshape(count, pack_all.shape[2]).astype(BF16)
    qin[...] = small[:, :rank]
    new_key[...] = jnp.concatenate(
        [small[:, rank : rank + LATENT + ROTARY], jnp.zeros((count, ROTARY), BF16)], axis=1
    )

    def attend(query, extra):
        queries = query[:, :LATENT]
        rotated = query[:, LATENT : LATENT + ROTARY]
        tops = []
        for score, held, turn, device in (
            (score_a, cache, rotary, me),
            (score_b, cache_o, rotary_o, partner),
        ):
            part = (matmul_t(queries, held[...]) + matmul(rotated, turn[...])) * scale
            place = lax.broadcasted_iota(jnp.int32, (rows, span), 1)
            part = jnp.where(place < limit[...] - device * span, part, NEG)
            score[...] = part
            tops.append(jnp.max(part, axis=1, keepdims=True))
        top = jnp.maximum(tops[0], tops[1])
        if extra:
            own_score = matmul_t(query, new_key[...]) * scale
            own_score = jnp.where(mask[...] > 0, own_score, NEG)
            top = jnp.maximum(top, jnp.max(own_score, axis=1, keepdims=True))
        shift = jnp.where(top > 0.5 * NEG, top, 0.0)
        total = jnp.zeros((rows, 1), F32)
        mixed = jnp.zeros((rows, LATENT), F32)
        for score, held in ((score_a, cache), (score_b, cache_o)):
            share = jnp.exp(score[...] - shift)
            total = total + jnp.sum(share, axis=1, keepdims=True)
            mixed = mixed + matmul(share.astype(BF16), held[...])
        if extra:
            share = jnp.exp(own_score - shift)
            total = total + jnp.sum(share, axis=1, keepdims=True)
            mixed = mixed + matmul(share.astype(BF16), new_key[:, :LATENT])
        return top, total, mixed

    lane = lax.broadcasted_iota(jnp.int32, (rows, 128), 1)

    def query_copy(o, g):
        peer = lax.bitwise_xor(me, 2 * (o + 1))
        return remote(q.at[g], q_all.at[o, g], qs.at[o, g], qr.at[o, g], "ctx", peer)

    def own_group(g, carry):
        for copy in group_copies(g):
            copy.wait()
        for i in range(2):
            h = g * 2 + i
            weights = key_all[:, h].reshape(latent, NOPE_DIM).astype(F32)
            weights = (weights + matmul(down_l[...], up_l[h, :, :NOPE_DIM])).astype(BF16)
            delta = matmul(down_q[...], up_q[h])
            base = plain_all[:, h].reshape(rank, NOPE_DIM).astype(F32)
            merged = (base + delta[:, :NOPE_DIM]).astype(BF16)
            absorbed = matmul_t(merged, weights).astype(BF16)
            lines = pl.ds(i * count, count)
            q[g, lines, :LATENT] = matmul(qin[...], absorbed).astype(BF16)
            halves = turned_all[:, h].astype(F32)
            base = jnp.concatenate([halves[:, :, :ROTARY], halves[:, :, ROTARY:]], axis=1)
            merged = (base.reshape(rank, ROTARY) + delta[:, NOPE_DIM:]).astype(BF16)
            raw = matmul(qin[...], merged)
            swapped = jnp.concatenate([raw[:, ROTARY // 2 :], raw[:, : ROTARY // 2]], axis=1)
            spun = raw * cosine[...] + swapped * sine[...]
            q[g, lines, LATENT:] = jnp.concatenate([spun, jnp.zeros_like(spun)], axis=1).astype(BF16)
        for o in range(chips - 2, -1, -1):
            query_copy(o, g).start()

        @pl.when(g == 0)
        def _():
            for copy in swaps:
                copy.wait()

        top, total, mixed = attend(q[g], True)
        kept[g] = mixed
        s_own[g] = jnp.where(lane == 0, top, total)
        return carry

    lax.fori_loop(0, groups, own_group, 0)

    def return_copies(o, g):
        peer = lax.bitwise_xor(me, 2 * (o + 1))
        return (
            remote(o_send.at[o, g], o_all.at[o, g], os_.at[o, g], or_.at[o, g], "ctx", peer),
            remote(s_send.at[o, g], s_all.at[o, g], ss.at[o, g], sr.at[o, g], "ctx", peer),
        )

    def peer_group(t, carry):
        g = t // (chips - 1)
        o = chips - 2 - t % (chips - 1)
        query_copy(o, g).wait()
        top, total, mixed = attend(q_all[o, g], False)
        o_send[o, g] = mixed.astype(BF16)
        s_send[o, g] = jnp.where(lane == 0, top, total)
        for copy in return_copies(o, g):
            copy.start()
        return carry

    lax.fori_loop(0, groups * (chips - 1), peer_group, 0)
    for copy in values:
        copy.wait()
    for g in range(groups):
        for o in range(chips - 2, -1, -1):
            for copy in return_copies(o, g):
                copy.wait()
        parts = [s_own[g]] + [s_all[o, g] for o in range(chips - 1)]
        best = functools.reduce(jnp.maximum, [part[:, :1] for part in parts])
        total = jnp.zeros((rows, 1), F32)
        mixed = jnp.zeros((rows, LATENT), F32)
        for index, part in enumerate(parts):
            factor = jnp.exp(part[:, :1] - best)
            total = total + part[:, 1:2] * factor
            block = kept[g] if index == 0 else o_all[index - 1, g].astype(F32)
            mixed = mixed + block * factor
        kept[g] = mixed / total
        for i in range(2):
            h = g * 2 + i
            width = val_all.shape[3]
            weights = val_all[:, h].reshape(latent, width).astype(F32)
            weights = (weights + matmul(down_l[...], up_l[h, :, NOPE_DIM:])).astype(BF16)
            piece[:, h * width : (h + 1) * width] = jnp.dot(
                kept[g, i * count : (i + 1) * count, :],
                weights.astype(F32),
                precision=lax.Precision.HIGHEST,
                preferred_element_type=F32,
            ).astype(BF16)

    copies = []
    for o in order:
        copy = remote(piece, pieces.at[mine], hs.at[o], hr.at[o], "ctx", peers[o - 1])
        copy.start()
        copies.append(copy)
    pieces[mine] = piece[...]
    for copy in loads:
        copy.wait()
    for copy in copies:
        copy.wait()
    total = matmul(pieces[0], wide[:depth])
    for g in range(1, n):
        total = total + matmul(pieces[g], wide[g * depth : (g + 1) * depth])
    band = total.shape[0] // nz
    for b in range(nz):
        partial[b] = total[b * band : (b + 1) * band]
    copies = []
    for o in range(1, nz):
        plane = planes[o - 1]
        copy = remote(partial.at[plane], landed.at[o - 1], zs.at[o - 1], zr.at[o - 1], "head", plane)
        copy.start()
        copies.append(copy)
    for copy in copies:
        copy.wait()
    result = partial[z]
    for o in range(nz - 1):
        result = result + landed[o]
    out[...] = result.astype(BF16)


def on_device_split(
    n,
    nz,
    query_input,
    new_latent,
    new_rotary,
    lengths,
    adapter_index,
    query_up,
    latent_up,
    query_adapter_down,
    query_adapter_up,
    latent_adapter_down,
    latent_adapter_up,
    cache_latent,
    cache_rotary,
    output_weight,
):
    chips = n // 2
    steps, local_rows, rank = query_input.shape
    band = local_rows * n // nz
    heads = query_up.shape[1]
    hd = heads // n
    groups = hd // 2
    slab = query_up.shape[0]
    half = slab // 2
    latent_slab = latent_up.shape[0]
    value_dim = latent_up.shape[2] - NOPE_DIM
    model = output_weight.shape[1]
    count = steps * local_rows * n
    me = lax.axis_index("ctx")
    first_head = block_of(me, chips) * hd

    plain = jnp.transpose(query_up[:, :, :NOPE_DIM], (1, 0, 2)).reshape(n, hd, slab, NOPE_DIM)
    turned = jnp.transpose(query_up[:, :, NOPE_DIM:], (1, 0, 2))
    turned = jnp.concatenate([turned[:, :half], turned[:, half:]], axis=2)
    turned = turned.reshape(n, hd, half, 2 * ROTARY)
    latents = jnp.transpose(latent_up, (1, 0, 2)).reshape(n, hd, latent_slab, latent_up.shape[2])
    key, val = latents[..., :NOPE_DIM], latents[..., NOPE_DIM:]
    small = jnp.concatenate([query_input, new_latent, new_rotary], axis=2).astype(F32)
    small = small.reshape(steps * local_rows, small.shape[2])
    pack = jnp.pad(small, ((0, 0), (0, -small.shape[1] % 128)))

    spread = lambda value: jnp.broadcast_to(value, (n, steps, local_rows)).reshape(count)
    step_of = spread(jnp.arange(steps, dtype=jnp.int32)[None, :, None])
    row_of = spread(
        jnp.arange(n * local_rows, dtype=jnp.int32).reshape(n, 1, local_rows)
    )
    length_of = spread(lengths.reshape(n, 1, local_rows))
    position = (length_of + step_of).astype(F32)[:, None]
    freq = jnp.exp(
        jnp.arange(ROTARY // 2, dtype=F32) * (-math.log(10000.0) / (ROTARY // 2))
    )
    angle = position * freq
    cosine = jnp.concatenate([jnp.cos(angle)] * 2, axis=1)
    sine = jnp.concatenate([-jnp.sin(angle), jnp.sin(angle)], axis=1)
    mask = (row_of[:, None] == row_of[None, :]) & (step_of[None, :] <= step_of[:, None])
    mask = jnp.tile(mask.astype(jnp.int32), (2, 1))
    limit = jnp.tile(length_of[:, None], (2, 1))

    chosen_query = adapter_index[0]
    chosen_latent = adapter_index[1]
    pick = lambda value, index: lax.dynamic_index_in_dim(value, index, 0, keepdims=False)
    down_q = pick(query_adapter_down, chosen_query)
    down_l = pick(latent_adapter_down, chosen_latent)
    width_r = down_q.shape[1]

    def own_heads(value, index):
        taken = lax.dynamic_slice(
            value, (index, 0, first_head, 0), (1, width_r, hd, value.shape[3])
        )[0]
        return jnp.transpose(taken, (1, 0, 2))

    up_q = own_heads(query_adapter_up, chosen_query)
    up_l = own_heads(latent_adapter_up, chosen_latent)

    key_width = LATENT + 2 * ROTARY
    lines = 2 * count
    others = chips - 1
    span = cache_latent.shape[0]
    dma = lambda *number: pltpu.SemaphoreType.DMA(number)
    store = lambda kind, *shape: pltpu.VMEM(shape, kind)
    result = pl.pallas_call(
        functools.partial(fused_kernel, n, chips, nz, hd),
        out_shape=jax.ShapeDtypeStruct((count // nz, model), BF16),
        in_specs=[anywhere()] * 5 + [vmem()] * 2 + [anywhere()] + [vmem()] * 8,
        out_specs=vmem(),
        scratch_shapes=[
            store(BF16, *key.shape),
            store(BF16, *plain.shape),
            store(BF16, *turned.shape),
            store(F32, n, *pack.shape),
            store(BF16, *val.shape),
            store(BF16, *cache_latent.shape),
            store(BF16, *cache_rotary.shape),
            store(BF16, *output_weight.shape),
            store(BF16, groups, lines, key_width),
            store(BF16, others, groups, lines, key_width),
            store(BF16, others, groups, lines, LATENT),
            store(BF16, others, groups, lines, LATENT),
            store(F32, others, groups, lines, 128),
            store(F32, others, groups, lines, 128),
            store(F32, groups, lines, 128),
            store(F32, lines, span),
            store(F32, lines, span),
            store(F32, groups, lines, LATENT),
            store(BF16, count, hd * value_dim),
            store(BF16, n, count, hd * value_dim),
            store(F32, nz, count // nz, model),
            store(F32, nz - 1, count // nz, model),
            store(BF16, count, rank),
            store(BF16, count, key_width),
        ]
        + [dma(n)] * 2
        + [dma(groups, n)] * 4
        + [dma(n)] * 4
        + [dma(2)] * 2
        + [dma(others, groups)] * 6
        + [dma(n)] * 2
        + [dma(nz - 1)] * 2
        + [dma(5), dma(n)],
        compiler_params=pltpu.CompilerParams(
            collective_id=0, has_side_effects=True, vmem_limit_bytes=VMEM_LIMIT
        ),
        name="fused",
    )(
        key, plain, turned, pack, val, cache_latent, cache_rotary, output_weight,
        down_q, up_q, down_l, up_l, cosine, sine, limit, mask,
    )
    devices = band // local_rows
    result = result.reshape(devices, steps, local_rows, model)
    return jnp.transpose(result, (1, 0, 2, 3)).reshape(steps, band, model)


def on_device(n, nz, *arrays):
    rows = arrays[0].shape[1] * n
    heads = arrays[5].shape[1]
    power = n >= 4 and n & (n - 1) == 0
    if power and nz > 1 and heads % (2 * n) == 0 and rows % nz == 0 and rows // nz % arrays[0].shape[1] == 0 and rows * arrays[0].shape[0] // nz % 16 == 0:
        return on_device_split(n, nz, *arrays)
    return on_device_general(*arrays)


def solution(mesh):
    placed = (
        P(None, "ctx", None),
        P(None, "ctx", None),
        P(None, "ctx", None),
        P(),
        P(),
        P("ctx", "head", None),
        P("ctx", "head", None),
        P(),
        P(None, None, "head", None),
        P(),
        P(None, None, "head", None),
        P("ctx", None),
        P(None, "ctx"),
        P("head", "ctx"),
    )
    return jax.shard_map(
        functools.partial(on_device, mesh.shape["ctx"], mesh.shape["head"]),
        mesh=mesh, in_specs=placed, out_specs=P(None, "head", "ctx"), check_vma=False
    )
```
